512 devices in a mesh: segment: 4 (over x), blk: 128 (over z, y, core).
Axes of the slice: x: 4, y: 8, z: 8, core: 2. Of those that a mesh axis runs over, the one named last changes fastest.
Arguments:
- inputs: bfloat16 [32, 65536], P('segment', 'blk'), may hold values from 0 to 24
- weights: bfloat16 [8, 512, 2048, 128], P('segment', 'blk'), may hold values from -0.1875 to 0.1875
- biases: float32 [8, 65536], P('segment', 'blk'), may hold values from -32 to 32
- sources: int32 [8, 512, 16], P('segment', 'blk'), may hold values from 0 to 511, as said below
- send_slot: int32 [8, 128, 128, 1], P('segment', 'blk'), may hold values from 0 to 4, as said below
Outputs:
- activations_out: bfloat16 [32, 65536], P('segment', 'blk')
The draws below stay inside these ranges and needn't reach their ends.
Inputs may be any that keep to these rules, and one draw needn't show every extreme that they name: `sources`: the 16 ids of one output block are distinct and no two of them share both owner g // 4 and residue g % 1; every id g of an output block owned by device d equals p * 4 + send_slot[l, p, d, g % 1] with p = g // 4. send_slot[l, p, d, s] is 4 where device d reads no block of device p with residue s in layer l, else a local block index whose residue modulo 1 is s.
All inputs are finite; a program needn't handle non-finite values.
Results may differ from the reference program's by a relative error of at most 0.011.
Values may be sent and summed in bfloat16 or wider, within the bound.
A program may use at most 64 MiB of HBM per device.

```python
import jax
import jax.numpy as jnp
from jax import lax

BLOCK = 128
COLS_DEV = 4
IN_BLK = 16
NB = 512
NEURONS = 65536
LAYERS = 8
ROWS = 32
CAP = 1
N_BLK = 128


def routing(key):
    folded = jax.random.fold_in(key, 7)
    seed_local, seed_columns = jax.random.split(folded)
    residue = jnp.arange(CAP, dtype=jnp.int32)[None, None, None, :]
    local_pick = residue + CAP * jax.random.randint(seed_local, (LAYERS, N_BLK, N_BLK, CAP), 0, COLS_DEV // CAP)
    local_pick = local_pick.at[:, 0, 0, CAP - 1].set(COLS_DEV - 1)
    subkeys = jax.random.split(seed_columns, LAYERS * NB)
    picked = jax.vmap(lambda subkey: jax.random.permutation(subkey, N_BLK * CAP)[:IN_BLK])(subkeys)
    picked = picked.reshape(LAYERS, NB, IN_BLK).astype(jnp.int32)
    sender = picked // CAP
    slot_index = picked % CAP
    receiver = (jnp.arange(NB, dtype=jnp.int32) // COLS_DEV)[None, :, None]
    layer_ids = jnp.arange(LAYERS, dtype=jnp.int32)[:, None, None]
    chosen = local_pick[layer_ids, sender, receiver, slot_index]
    source_ids = sender * COLS_DEV + chosen
    in_use = jnp.zeros((LAYERS, N_BLK, N_BLK, CAP), jnp.int32).at[layer_ids, sender, receiver, slot_index].max(1)
    outgoing = jnp.where(in_use > 0, local_pick, COLS_DEV)
    return (source_ids.astype(jnp.int32), outgoing.astype(jnp.int32))


def draw_sources(key, part):
    return routing(key)[0]


def draw_send_slot(key, part):
    return routing(key)[1]


def draw_biases(key, part):
    key = jax.random.fold_in(key, 11)
    seed_offset, seed_spread = jax.random.split(key, 2)
    offset = jax.random.uniform(seed_offset, (LAYERS, NB, 1), jnp.float32, -24.0, 24.0)
    spread = jax.random.uniform(seed_spread, (LAYERS, NB, BLOCK), jnp.float32, -6.0, 6.0)
    return (offset + spread).reshape(LAYERS, NEURONS).astype(jnp.float32)


def levels(key, dims, cuts, least, top_value):
    def one(axis_at, parts):
        steps = jax.random.uniform(jax.random.fold_in(jax.random.fold_in(key, 6), axis_at), (parts,), jnp.float32, least / len(cuts), top_value / len(cuts))
        return jnp.repeat(jnp.exp(steps), dims[axis_at] // parts).reshape((-1,) + (1,) * (len(dims) - axis_at - 1))

    gain = one(*cuts[0])
    for cut in cuts[1:]:
        gain = gain * one(*cut)
    return gain


def normal_values(rng, dims, deviation, limit, cuts=(), held_as=jnp.bfloat16):
    values = deviation * jax.random.normal(rng, dims, jnp.float32)
    if cuts:
        values = values * levels(rng, dims, cuts, -0.22, 0.18)
    return jnp.clip(values, -limit, limit).astype(held_as)


def setup_inputs(seed: int = 0) -> dict:
    streams_of = jax.random.split(jax.random.key(seed), 6)
    return {
        "inputs": jnp.clip(24.0 * jax.random.uniform(streams_of[0], (ROWS, NEURONS), jnp.float32) ** levels(streams_of[0], (ROWS, NEURONS), ((0, 4), (1, 128)), -0.2, 0.2), 0.0, 24.0).astype(jnp.bfloat16),
        "weights": normal_values(streams_of[1], (LAYERS, NB, IN_BLK * BLOCK, BLOCK), (IN_BLK * BLOCK // 2) ** -0.5, 0.1875, ((0, 4), (1, 128))),
        "biases": draw_biases(jax.random.fold_in(streams_of[5], 71), 0),
        "sources": draw_sources(jax.random.fold_in(streams_of[5], 71), 0),
        "send_slot": draw_send_slot(jax.random.fold_in(streams_of[5], 71), 0),
    }


def reference(inputs, weights, biases, sources, send_slot):
    row_count = inputs.shape[0]
    current = inputs
    receiver = (jnp.arange(NB, dtype=jnp.int32) // COLS_DEV)[:, None]
    for layer_index in range(LAYERS):
        ids = sources[layer_index]
        owners = (ids // COLS_DEV).astype(jnp.int32)
        local_index = send_slot[layer_index][owners, receiver, ids % CAP]
        block_ids = (owners * COLS_DEV + local_index).astype(jnp.int32)
        block_pool = current.reshape(row_count, NB, BLOCK)
        layer_weights = weights[layer_index].reshape(NB, IN_BLK, BLOCK, BLOCK)

        def contract(pair):
            wanted, tiles = pair
            picked = jnp.take(block_pool, wanted, axis=1).astype(jnp.float32)
            return jnp.einsum("rkn,knm->rm", picked, tiles.astype(jnp.float32))

        summed = lax.map(contract, (block_ids, layer_weights))
        summed = jnp.transpose(summed, (1, 0, 2)).reshape(row_count, NEURONS)
        current = jnp.clip(summed + biases[layer_index][None, :], 0.0, 32.0).astype(jnp.bfloat16)
    return (current.astype(jnp.float32) / 32.0).astype(jnp.bfloat16)
```

```python
import jax
import jax.numpy as jnp
from jax import lax
from jax.experimental import pallas as pl
from jax.experimental.pallas import tpu as pltpu
from jax.sharding import PartitionSpec as P

MESH = pl.DeviceIdType.MESH
CEILING = 32.0
SIDE = 8
READERS = 2 * SIDE * SIDE
SECTIONS = 4
BLOCKS = 4
FAN = 16
ROWS = 8
WIDTH = 128


FAR = (4, 3, 5, 2, 6, 1, 7, 0)


def kernel(
    inputs_ref, weights_ref, biases_ref, sources_ref, slots_ref, slot_rows_ref, out_ref,
    held, first_0, first_1, first_2, first_3, second_0, second_1, second_2, second_3,
    first_out, second_out, start_out, tiles, result, landed,
    slots_in, start_slots, next_slots,
    first_recv, second_recv, first_send, second_send, start_send,
    tile_sem, slot_send, slot_recv, table_sem, land_send, land_recv, ready,
):
    first_in = (first_0, first_1, first_2, first_3)
    second_in = (second_0, second_1, second_2, second_3)
    section = lax.axis_index("segment")
    me = lax.axis_index("blk")
    z, y, core = me // (2 * SIDE), (me // 2) % SIDE, me % 2
    last = SECTIONS - 1

    places = [((y + dy) % SIDE) * 2 + c for dy in FAR for c in (0, 1)]

    def row_of(step):
        half = (step + 1) // 2
        return (z + SIDE // 2 + jnp.where(step % 2 == 1, -half, half)) % SIDE * (2 * SIDE)

    def each_reader(act):
        def some(step, carry):
            row = row_of(step)
            for place in places:
                act(row + place)
            return carry

        lax.fori_loop(0, SIDE - 1, some, 0)
        for place in places[:-2]:
            act(z * (2 * SIDE) + place)
        act(me + 1 - 2 * core)

    fetch = pltpu.make_async_copy(weights_ref, tiles, tile_sem)
    fetch.start()

    barrier = pltpu.get_barrier_semaphore()
    each_reader(
        lambda reader: pl.semaphore_signal(
            barrier, inc=1, device_id=(section, reader), device_id_type=MESH
        )
    )
    for step in range(1, SECTIONS):
        other = (section + step) % SECTIONS
        pl.semaphore_signal(barrier, inc=1, device_id=(other, me), device_id_type=MESH)

    for block in range(BLOCKS):
        held[block] = inputs_ref[:, block * WIDTH : (block + 1) * WIDTH]

    pl.semaphore_wait(barrier, READERS - 1 + SECTIONS - 1)

    slot_copies = []
    for step in range(1, SECTIONS):
        other = (section + step) % SECTIONS
        pl.semaphore_signal(ready.at[step - 1], inc=1, device_id=(other, me), device_id_type=MESH)
        copy = pltpu.make_async_remote_copy(
            src_ref=slot_rows_ref,
            dst_ref=slots_in.at[step - 1],
            send_sem=slot_send.at[step - 1],
            recv_sem=slot_recv.at[step - 1],
            device_id=(other, me),
            device_id_type=MESH,
        )
        copy.start()
        slot_copies.append(copy)

    def exchange(slot_of, outgoing, target, arriving, send_sem, recv_sem, own):
        def pick(row):
            for place in range(2 * SIDE):
                slot = jnp.minimum(slot_of(row + place), BLOCKS - 1)
                outgoing[row + place] = held[slot]

        def post(reader):
            pltpu.make_async_remote_copy(
                src_ref=outgoing.at[reader],
                dst_ref=arriving.at[me],
                send_sem=send_sem,
                recv_sem=recv_sem,
                device_id=(target, reader),
                device_id_type=MESH,
            ).start()

        def some(step, carry):
            row = row_of(step)
            pick(row)
            for place in places:
                post(row + place)
            return carry

        lax.fori_loop(0, SIDE - 1, some, 0)
        row = z * (2 * SIDE)
        pick(row)
        for place in places[:-2]:
            post(row + place)
        post(me + 1 - 2 * core)
        if own:
            arriving[me] = outgoing[me]
        else:
            post(me)

    def landed_bytes(arriving, count, sem):
        part = arriving.at[pl.ds(0, count)]
        pltpu.make_async_copy(part, part, sem).wait()

    def layer(index, arriving):
        for block in range(BLOCKS):
            parts = [arriving[sources_ref[index, block, k] // BLOCKS] for k in range(FAN)]
            summed = jnp.dot(
                jnp.concatenate(parts, axis=1),
                tiles[index, block],
                preferred_element_type=jnp.float32,
            )
            shifted = summed + biases_ref[index : index + 1, block * WIDTH : (block + 1) * WIDTH]
            held[block] = jnp.clip(shifted, 0.0, CEILING).astype(jnp.bfloat16)

    @pl.when(section == 0)
    def _():
        exchange(
            lambda reader: slots_ref[0, reader],
            start_out, 0, first_0, start_send, first_recv.at[0], True,
        )

    for step in range(1, SECTIONS):
        pl.semaphore_wait(ready.at[step - 1], 1)
        slot_copies[step - 1].wait_recv()

    for batch in range(1, SECTIONS):

        @pl.when(section == batch)
        def _():
            table = pltpu.make_async_copy(slots_in.at[batch - 1], start_slots, table_sem)
            table.start()
            table.wait()
            exchange(
                lambda reader: start_slots[0, reader],
                start_out, 0, first_in[batch], start_send, first_recv.at[batch], False,
            )

    table = pltpu.make_async_copy(slots_in.at[SECTIONS - 2], next_slots, table_sem)
    table.start()
    table.wait()
    fetch.wait()

    def first(batch):
        if batch == 0:

            @pl.when(section == 0)
            def _():
                landed_bytes(first_0, READERS - 1, first_recv.at[0])

            @pl.when(section > 0)
            def _():
                landed_bytes(first_0, READERS, first_recv.at[0])

        else:
            landed_bytes(first_in[batch], READERS, first_recv.at[batch])
        layer(0, first_in[batch])
        exchange(
            lambda reader: slots_ref[1, reader], second_out.at[batch], section,
            second_in[batch], second_send.at[batch], second_recv.at[batch], True,
        )

    def second(batch):
        landed_bytes(second_in[batch], READERS - 1, second_recv.at[batch])
        layer(1, second_in[batch])

        @pl.when(section < last)
        def _():
            exchange(
                lambda reader: next_slots[0, reader], first_out.at[batch], section + 1,
                first_in[batch], first_send.at[batch], first_recv.at[batch], False,
            )

        @pl.when(section == last)
        def _():
            for block in range(BLOCKS):
                scaled = held[block].astype(jnp.float32) * (1.0 / CEILING)
                result[batch, :, block * WIDTH : (block + 1) * WIDTH] = scaled.astype(jnp.bfloat16)
            if batch < last:
                pltpu.make_async_remote_copy(
                    src_ref=result.at[batch],
                    dst_ref=landed,
                    send_sem=land_send,
                    recv_sem=land_recv,
                    device_id=(batch, me),
                    device_id_type=MESH,
                ).start()

    for step in range(SECTIONS + 1):
        if step < SECTIONS:
            first(step)
        if step > 0:
            second(step - 1)

    for copy in slot_copies:
        copy.wait_send()

    @pl.when(section == 0)
    def _():
        landed_bytes(start_out, READERS - 1, start_send)

    @pl.when(section > 0)
    def _():
        landed_bytes(start_out, READERS, start_send)

    for batch in range(SECTIONS):
        landed_bytes(second_out.at[batch], READERS - 1, second_send.at[batch])

    @pl.when(section < last)
    def _():
        for batch in range(SECTIONS):
            landed_bytes(first_out.at[batch], READERS, first_send.at[batch])
        pltpu.make_async_copy(landed, landed, land_recv).wait()
        out_ref[...] = landed[...]

    @pl.when(section == last)
    def _():
        sent = result.at[pl.ds(0, SECTIONS - 1)]
        pltpu.make_async_copy(sent, sent, land_send).wait()
        out_ref[...] = result[last]


def per_device(inputs, weights, biases, sources, send_slot):
    slots = send_slot.reshape(2, READERS)
    vmem = pl.BlockSpec(memory_space=pltpu.VMEM)
    smem = pl.BlockSpec(memory_space=pltpu.SMEM)
    bf16 = jnp.bfloat16
    pool = (READERS, ROWS, WIDTH)
    dma = pltpu.SemaphoreType.DMA
    return pl.pallas_call(
        kernel,
        out_shape=jax.ShapeDtypeStruct((ROWS, BLOCKS * WIDTH), bf16),
        in_specs=[vmem, pl.BlockSpec(memory_space=pl.ANY), vmem, smem, smem, vmem],
        out_specs=vmem,
        scratch_shapes=[
            pltpu.VMEM((BLOCKS, ROWS, WIDTH), bf16),
            *[pltpu.VMEM(pool, bf16)] * (2 * SECTIONS),
            pltpu.VMEM((SECTIONS, *pool), bf16),
            pltpu.VMEM((SECTIONS, *pool), bf16),
            pltpu.VMEM(pool, bf16),
            pltpu.VMEM(weights.shape, bf16),
            pltpu.VMEM((SECTIONS, ROWS, BLOCKS * WIDTH), bf16),
            pltpu.VMEM((ROWS, BLOCKS * WIDTH), bf16),
            pltpu.VMEM((SECTIONS - 1, 2, READERS), jnp.int32),
            pltpu.SMEM((2, READERS), jnp.int32),
            pltpu.SMEM((2, READERS), jnp.int32),
            dma((SECTIONS,)),
            dma((SECTIONS,)),
            dma((SECTIONS,)),
            dma((SECTIONS,)),
            dma(()),
            dma(()),
            dma((SECTIONS - 1,)),
            dma((SECTIONS - 1,)),
            dma(()),
            dma(()),
            dma(()),
            pltpu.SemaphoreType.REGULAR((SECTIONS - 1,)),
        ],
        compiler_params=pltpu.CompilerParams(
            collective_id=0, has_side_effects=True, vmem_limit_bytes=40 * 2**20
        ),
        cost_estimate=pl.CostEstimate(flops=2**28, bytes_accessed=2**23, transcendentals=0),
    )(inputs, weights, biases, sources, slots, slots)


def solution(mesh):
    placed = (
        P("segment", "blk"),
        P("segment", "blk", None, None),
        P("segment", "blk"),
        P("segment", "blk", None),
        P("segment", "blk", None, None),
    )
    return jax.shard_map(
        per_device, mesh=mesh, in_specs=placed, out_specs=P("segment", "blk"), check_vma=False
    )
```

```python
import jax
import jax.numpy as jnp
from jax import lax
from jax.experimental import pallas as pl
from jax.experimental.pallas import tpu as pltpu
from jax.sharding import PartitionSpec as P

MESH = pl.DeviceIdType.MESH
CEILING = 32.0
SIDE = 8
READERS = 2 * SIDE * SIDE
SECTIONS = 4
BLOCKS = 4
FAN = 16
ROWS = 8
WIDTH = 128
NAMES = ("one", "two", "three", "four")


def kernel(
    inputs_hbm, weights_hbm, biases_hbm, sources_hbm, slots_hbm, out_ref,
    held, first_0, first_1, first_2, first_3, second_0, second_1, second_2, second_3,
    first_out, second_out, start_out, inputs_ref, tiles, biases_ref, sources_ref,
    slots_ref, slot_rows, start_rows, next_rows, start_slots, next_slots, result, landed,
    first_recv, second_recv, first_send, second_send, start_send,
    load_sem, row_send, start_row_recv, next_row_recv, table_sem, land_send, land_recv, hello,
):
    first_in = (first_0, first_1, first_2, first_3)
    second_in = (second_0, second_1, second_2, second_3)
    section = lax.axis_index("segment")
    me = lax.axis_index("blk")
    z, y, core = me // (2 * SIDE), (me // 2) % SIDE, me % 2
    last = SECTIONS - 1
    middle = SIDE // 2

    loads = [
        pltpu.make_async_copy(source, target, load_sem.at[i])
        for i, (source, target) in enumerate((
            (inputs_hbm, inputs_ref),
            (slots_hbm, slots_ref),
            (slots_hbm, slot_rows),
            (sources_hbm, sources_ref),
            (biases_hbm, biases_ref),
            (weights_hbm, tiles),
        ))
    ]
    for load in loads:
        load.start()

    def each_chip(act):
        def chip(dz, dy):
            row = (z + dz + SIDE) % SIDE * SIDE + (y + dy + SIDE) % SIDE
            act(2 * row)
            act(2 * row + 1)

        def some(total, carry):
            total = SIDE - total

            def pair(far_z, inner):
                far_y = total - far_z
                turn_z = jnp.logical_and(far_z > 0, far_z < middle)
                turn_y = jnp.logical_and(far_y > 0, far_y < middle)
                chip(far_z, far_y)

                @pl.when(jnp.logical_and(turn_z, turn_y))
                def _():
                    chip(-far_z, -far_y)

                @pl.when(turn_z)
                def _():
                    chip(-far_z, far_y)

                @pl.when(turn_y)
                def _():
                    chip(far_z, -far_y)

                return inner

            return lax.fori_loop(jnp.maximum(total - middle, 0), jnp.minimum(total, middle) + 1, pair, carry)

        lax.fori_loop(0, SIDE, some, 0)

    barrier = pltpu.get_barrier_semaphore()

    def greet(reader):
        pl.semaphore_signal(barrier, inc=1, device_id=(section, reader), device_id_type=MESH)

    sibling = me + 1 - 2 * core
    with jax.named_scope("enter"):

        @pl.when(section == 0)
        def _():
            for other in range(1, SECTIONS):
                pl.semaphore_signal(barrier, inc=1, device_id=(other, me), device_id_type=MESH)

        @pl.when(jnp.logical_and(section > 0, section < last))
        def _():
            pl.semaphore_signal(barrier, inc=1, device_id=(section + 1, me), device_id_type=MESH)

        each_chip(greet)
        greet(sibling)
        for load in loads[:3]:
            load.wait()
        for block in range(BLOCKS):
            held[block] = inputs_ref[:, block * WIDTH : (block + 1) * WIDTH]
        pl.semaphore_wait(barrier, READERS - 1 + jnp.minimum(section, 2))

    def send_rows(target, arriving, send_sem, recv_sem):
        pltpu.make_async_remote_copy(
            src_ref=slot_rows,
            dst_ref=arriving,
            send_sem=send_sem,
            recv_sem=recv_sem,
            device_id=(target, me),
            device_id_type=MESH,
        ).start()

    def full(ref, sem):
        pltpu.make_async_copy(ref, ref, sem).wait()

    def exchange(slot_of, outgoing, target, arriving, send_sem, recv_sem, own):
        def put(reader):
            outgoing[reader] = held[jnp.minimum(slot_of(reader), BLOCKS - 1)]

        def post(reader):
            put(reader)
            pltpu.make_async_remote_copy(
                src_ref=outgoing.at[reader],
                dst_ref=arriving.at[me],
                send_sem=send_sem,
                recv_sem=recv_sem,
                device_id=(target, reader),
                device_id_type=MESH,
            ).start()

        each_chip(post)
        post(sibling)
        if own:
            arriving[me] = held[jnp.minimum(slot_of(me), BLOCKS - 1)]
        else:
            post(me)

    def arrived(ref, count, sem):
        part = ref.at[pl.ds(0, count)]
        pltpu.make_async_copy(part, part, sem).wait()

    def layer(index, arriving):
        for block in range(BLOCKS):
            parts = [arriving[sources_ref[index, block, k] // BLOCKS] for k in range(FAN)]
            summed = jnp.dot(
                jnp.concatenate(parts, axis=1),
                tiles[index, block],
                preferred_element_type=jnp.float32,
            )
            shifted = summed + biases_ref[index : index + 1, block * WIDTH : (block + 1) * WIDTH]
            held[block] = jnp.clip(shifted, 0.0, CEILING).astype(jnp.bfloat16)

    def to_table(rows, table):
        copy = pltpu.make_async_copy(rows, table, table_sem)
        copy.start()
        copy.wait()

    with jax.named_scope("start"):

        @pl.when(section == 0)
        def _():
            exchange(
                lambda reader: slots_ref[0, reader],
                start_out, 0, first_0, start_send, first_recv.at[0], True,
            )
            full(next_rows, next_row_recv)
            send_rows(1, start_rows, row_send.at[0], start_row_recv)
            pl.semaphore_wait(hello.at[0], 1)
            send_rows(2, start_rows, row_send.at[1], start_row_recv)

        @pl.when(section > 0)
        def _():
            send_rows(section - 1, next_rows, row_send.at[0], next_row_recv)

        for batch in range(1, SECTIONS):

            @pl.when(section == batch)
            def _():
                if batch > 1:
                    pl.semaphore_signal(hello.at[batch - 2], inc=1, device_id=(0, me), device_id_type=MESH)
                full(start_rows, start_row_recv)
                to_table(start_rows, start_slots)
                exchange(
                    lambda reader: start_slots[0, reader],
                    start_out, 0, first_in[batch], start_send, first_recv.at[batch], False,
                )

        for load in loads[3:]:
            load.wait()

    def first(batch):
        name = NAMES[batch]
        with jax.named_scope("wait a " + name):
            if batch == 0:

                @pl.when(section == 0)
                def _():
                    arrived(first_0, READERS - 1, first_recv.at[0])

                @pl.when(section > 0)
                def _():
                    full(first_0, first_recv.at[0])

            else:
                full(first_in[batch], first_recv.at[batch])
        with jax.named_scope("layer a " + name):
            layer(0, first_in[batch])
        with jax.named_scope("send a " + name):
            exchange(
                lambda reader: slots_ref[1, reader], second_out.at[batch], section,
                second_in[batch], second_send.at[batch], second_recv.at[batch], True,
            )

    def second(batch):
        name = NAMES[batch]
        with jax.named_scope("wait b " + name):
            arrived(second_in[batch], READERS - 1, second_recv.at[batch])
        with jax.named_scope("layer b " + name):
            layer(1, second_in[batch])
        with jax.named_scope("send b " + name):

            @pl.when(section < last)
            def _():
                exchange(
                    lambda reader: next_slots[0, reader], first_out.at[batch], section + 1,
                    first_in[batch], first_send.at[batch], first_recv.at[batch], False,
                )

            @pl.when(section == last)
            def _():
                for block in range(BLOCKS):
                    scaled = held[block].astype(jnp.float32) * (1.0 / CEILING)
                    result[batch, :, block * WIDTH : (block + 1) * WIDTH] = scaled.astype(jnp.bfloat16)
                if batch < last:
                    pltpu.make_async_remote_copy(
                        src_ref=result.at[batch],
                        dst_ref=landed,
                        send_sem=land_send,
                        recv_sem=land_recv,
                        device_id=(batch, me),
                        device_id_type=MESH,
                    ).start()

    for step in range(SECTIONS + 1):
        if step < SECTIONS:
            first(step)
        if step == 0:

            @pl.when(section == 0)
            def _():
                pl.semaphore_wait(hello.at[1], 1)
                send_rows(3, start_rows, row_send.at[2], start_row_recv)
                to_table(next_rows, next_slots)

            @pl.when(jnp.logical_and(section > 0, section < last))
            def _():
                full(next_rows, next_row_recv)
                to_table(next_rows, next_slots)

        if step > 0:
            second(step - 1)

    with jax.named_scope("leave"):
        full(slot_rows, row_send.at[0])

        @pl.when(section == 0)
        def _():
            full(slot_rows, row_send.at[1])
            full(slot_rows, row_send.at[2])
            arrived(start_out, READERS - 1, start_send)

        @pl.when(section > 0)
        def _():
            full(start_out, start_send)

        for batch in range(SECTIONS):
            arrived(second_out.at[batch], READERS - 1, second_send.at[batch])

        @pl.when(section < last)
        def _():
            for batch in range(SECTIONS):
                full(first_out.at[batch], first_send.at[batch])
            full(landed, land_recv)
            out_ref[...] = landed[...]

        @pl.when(section == last)
        def _():
            full(result.at[pl.ds(0, SECTIONS - 1)], land_send)
            out_ref[...] = result[last]


def per_device(inputs, weights, biases, sources, send_slot):
    slots = send_slot.reshape(2, READERS)
    bf16 = jnp.bfloat16
    pool = (READERS, ROWS, WIDTH)
    dma = pltpu.SemaphoreType.DMA
    return pl.pallas_call(
        kernel,
        out_shape=jax.ShapeDtypeStruct((ROWS, BLOCKS * WIDTH), bf16),
        in_specs=[pl.BlockSpec(memory_space=pltpu.HBM)] * 5,
        out_specs=pl.BlockSpec(memory_space=pltpu.VMEM),
        scratch_shapes=[
            pltpu.VMEM((BLOCKS, ROWS, WIDTH), bf16),
            *[pltpu.VMEM(pool, bf16)] * (2 * SECTIONS),
            pltpu.VMEM((SECTIONS, *pool), bf16),
            pltpu.VMEM((SECTIONS, *pool), bf16),
            pltpu.VMEM(pool, bf16),
            pltpu.VMEM(inputs.shape, bf16),
            pltpu.VMEM(weights.shape, bf16),
            pltpu.VMEM(biases.shape, jnp.float32),
            pltpu.SMEM(sources.shape, jnp.int32),
            pltpu.SMEM(slots.shape, jnp.int32),
            pltpu.VMEM(slots.shape, jnp.int32),
            pltpu.VMEM(slots.shape, jnp.int32),
            pltpu.VMEM(slots.shape, jnp.int32),
            pltpu.SMEM(slots.shape, jnp.int32),
            pltpu.SMEM(slots.shape, jnp.int32),
            pltpu.VMEM((SECTIONS, ROWS, BLOCKS * WIDTH), bf16),
            pltpu.VMEM((ROWS, BLOCKS * WIDTH), bf16),
            dma((SECTIONS,)),
            dma((SECTIONS,)),
            dma((SECTIONS,)),
            dma((SECTIONS,)),
            dma(()),
            dma((6,)),
            dma((SECTIONS - 1,)),
            dma(()),
            dma(()),
            dma(()),
            dma(()),
            dma(()),
            pltpu.SemaphoreType.REGULAR((2,)),
        ],
        compiler_params=pltpu.CompilerParams(
            collective_id=0, has_side_effects=True, vmem_limit_bytes=60 * 2**20
        ),
        cost_estimate=pl.CostEstimate(flops=2**28, bytes_accessed=2**23, transcendentals=0),
    )(inputs, weights, biases, sources, slots)


def solution(mesh):
    placed = (
        P("segment", "blk"),
        P("segment", "blk", None, None),
        P("segment", "blk"),
        P("segment", "blk", None),
        P("segment", "blk", None, None),
    )
    return jax.shard_map(
        per_device, mesh=mesh, in_specs=placed, out_specs=P("segment", "blk"), check_vma=False
    )
```

```python
import jax
import jax.numpy as jnp
from jax import lax
from jax.experimental import pallas as pl
from jax.experimental.pallas import tpu as pltpu
from jax.sharding import PartitionSpec as P

MESH = pl.DeviceIdType.MESH
CEILING = 32.0
SIDE = 8
READERS = 2 * SIDE * SIDE
SECTIONS = 4
BLOCKS = 4
FAN = 16
ROWS = 8
WIDTH = 128
FAR = (4, 3, 5, 2, 6, 1, 7, 0)
RELAYED = 2 * SIDE - 1


def kernel(
    inputs_hbm, weights_hbm, biases_hbm, sources_hbm, slots_hbm, out_ref,
    held, first_0, first_1, first_2, first_3, second_0, second_1, second_2, second_3,
    first_out, second_out, start_out, inputs_ref, tiles, biases_ref, sources_ref,
    slots_ref, slot_rows, start_rows, next_rows, start_slots, next_slots, result, landed,
    first_recv, second_recv, first_send, second_send, start_send,
    relay_in, relay_recv, bundle_send, relay_send,
    load_sem, row_send, start_row_recv, next_row_recv, table_sem, land_send, land_recv, hello,
):
    first_in = (first_0, first_1, first_2, first_3)
    second_in = (second_0, second_1, second_2, second_3)
    section = lax.axis_index("segment")
    me = lax.axis_index("blk")
    z, y, core = me // (2 * SIDE), (me // 2) % SIDE, me % 2
    last = SECTIONS - 1
    middle = SIDE // 2
    other = 1 - core
    across_z, across_y = (z + middle) % SIDE, (y + middle) % SIDE

    loads = [
        pltpu.make_async_copy(source, target, load_sem.at[i])
        for i, (source, target) in enumerate((
            (inputs_hbm, inputs_ref),
            (slots_hbm, slots_ref),
            (slots_hbm, slot_rows),
            (sources_hbm, sources_ref),
            (biases_hbm, biases_ref),
            (weights_hbm, tiles),
        ))
    ]
    for load in loads:
        load.start()

    def place(at_z, at_y, at_core):
        return (at_z * SIDE + at_y) * 2 + at_core

    def each_chip(act):
        def some(step, carry):
            total = SIDE - step

            def pair(far_z, inner):
                far_y = total - far_z
                turn_z = jnp.logical_and(far_z > 0, far_z < middle)
                turn_y = jnp.logical_and(far_y > 0, far_y < middle)
                near = jnp.logical_and(far_z < middle, far_y < middle)

                def chip(dz, dy):
                    at_z, at_y = (z + dz + SIDE) % SIDE, (y + dy + SIDE) % SIDE
                    act(at_z, at_y, core)

                    @pl.when(near)
                    def _():
                        act(at_z, at_y, other)

                chip(far_z, far_y)

                @pl.when(jnp.logical_and(turn_z, turn_y))
                def _():
                    chip(-far_z, -far_y)

                @pl.when(turn_z)
                def _():
                    chip(-far_z, far_y)

                @pl.when(turn_y)
                def _():
                    chip(far_z, -far_y)

                return inner

            return lax.fori_loop(jnp.maximum(total - middle, 0), jnp.minimum(total, middle) + 1, pair, carry)

        lax.fori_loop(0, SIDE, some, 0)

    barrier = pltpu.get_barrier_semaphore()

    def greet(step, carry):
        reader = (me + step) % READERS
        pl.semaphore_signal(barrier, inc=1, device_id=(section, reader), device_id_type=MESH)
        return carry


    @pl.when(section == 0)
    def _():
        for later in range(1, SECTIONS):
            pl.semaphore_signal(barrier, inc=1, device_id=(later, me), device_id_type=MESH)

    @pl.when(jnp.logical_and(section > 0, section < last))
    def _():
        pl.semaphore_signal(barrier, inc=1, device_id=(section + 1, me), device_id_type=MESH)

    lax.fori_loop(1, READERS, greet, 0)
    for load in loads[:3]:
        load.wait()
    for block in range(BLOCKS):
        held[block] = inputs_ref[:, block * WIDTH : (block + 1) * WIDTH]
    pl.semaphore_wait(barrier, READERS - 1 + jnp.minimum(section, 2))

    def send_rows(target, arriving, send_sem, recv_sem):
        pltpu.make_async_remote_copy(
            src_ref=slot_rows,
            dst_ref=arriving,
            send_sem=send_sem,
            recv_sem=recv_sem,
            device_id=(target, me),
            device_id_type=MESH,
        ).start()

    def full(ref, sem):
        pltpu.make_async_copy(ref, ref, sem).wait()

    def exchange(index, slot_of, outgoing, target, arriving, send_sem, recv_sem, own):
        def pick(at_z, at_y, at_core):
            return held[jnp.minimum(slot_of(place(at_z, at_y, at_core)), BLOCKS - 1)]

        def put(at_z, at_y, at_core):
            outgoing[at_z, at_y, at_core] = pick(at_z, at_y, at_core)

        def post(at_z, at_y, at_core):
            put(at_z, at_y, at_core)
            pltpu.make_async_remote_copy(
                src_ref=outgoing.at[at_z, at_y, at_core],
                dst_ref=arriving.at[me],
                send_sem=send_sem,
                recv_sem=recv_sem,
                device_id=(target, place(at_z, at_y, at_core)),
                device_id_type=MESH,
            ).start()

        for step in range(SIDE):
            put(step, across_y, other)
        for step in range(SIDE):
            put(across_z, step, other)
        bundles = (
            (outgoing.at[:, across_y, other], place(z, (y + SIDE - 1) % SIDE, core)),
            (outgoing.at[across_z, :, other], place((z + SIDE - 1) % SIDE, y, core)),
        )
        for side, (bundle, relay_at) in enumerate(bundles):
            pltpu.make_async_remote_copy(
                src_ref=bundle,
                dst_ref=relay_in.at[index, side],
                send_sem=bundle_send.at[index],
                recv_sem=relay_recv.at[index, side],
                device_id=(section, relay_at),
                device_id_type=MESH,
            ).start()
        each_chip(post)
        post(z, y, other)
        if own:
            arriving[me] = pick(z, y, core)
        else:
            post(z, y, core)

        def forward(side, step, origin, at_z, at_y):
            pltpu.make_async_remote_copy(
                src_ref=relay_in.at[index, side, step],
                dst_ref=arriving.at[origin],
                send_sem=relay_send.at[index],
                recv_sem=recv_sem,
                device_id=(target, place(at_z, at_y, other)),
                device_id_type=MESH,
            ).start()

        full(relay_in.at[index, 0], relay_recv.at[index, 0])
        for far in FAR:
            step = (z + far) % SIDE
            forward(0, step, place(z, (y + 1) % SIDE, core), step, (y + 1 + middle) % SIDE)
        full(relay_in.at[index, 1], relay_recv.at[index, 1])
        for far in FAR[1:]:
            step = (y + far) % SIDE
            forward(1, step, place((z + 1) % SIDE, y, core), (z + 1 + middle) % SIDE, step)

    def arrived(ref, count, sem):
        part = ref.at[pl.ds(0, count)]
        pltpu.make_async_copy(part, part, sem).wait()

    def layer(index, arriving):
        for block in range(BLOCKS):
            parts = [arriving[sources_ref[index, block, k] // BLOCKS] for k in range(FAN)]
            summed = jnp.dot(
                jnp.concatenate(parts, axis=1),
                tiles[index, block],
                preferred_element_type=jnp.float32,
            )
            shifted = summed + biases_ref[index : index + 1, block * WIDTH : (block + 1) * WIDTH]
            held[block] = jnp.clip(shifted, 0.0, CEILING).astype(jnp.bfloat16)

    def to_table(rows, table):
        copy = pltpu.make_async_copy(rows, table, table_sem)
        copy.start()
        copy.wait()


    @pl.when(section == 0)
    def _():
        exchange(
            0, lambda reader: slots_ref[0, reader],
            start_out, 0, first_0, start_send, first_recv.at[0], True,
        )
        full(next_rows, next_row_recv)
        send_rows(1, start_rows, row_send.at[0], start_row_recv)
        pl.semaphore_wait(hello.at[0], 1)
        send_rows(2, start_rows, row_send.at[1], start_row_recv)

    @pl.when(section > 0)
    def _():
        send_rows(section - 1, next_rows, row_send.at[0], next_row_recv)

    for batch in range(1, SECTIONS):

        @pl.when(section == batch)
        def _():
            if batch > 1:
                pl.semaphore_signal(hello.at[batch - 2], inc=1, device_id=(0, me), device_id_type=MESH)
            full(start_rows, start_row_recv)
            to_table(start_rows, start_slots)
            exchange(
                0, lambda reader: start_slots[0, reader],
                start_out, 0, first_in[batch], start_send, first_recv.at[batch], False,
            )

    for load in loads[3:]:
        load.wait()

    def first(batch):
        if batch == 0:

            @pl.when(section == 0)
            def _():
                arrived(first_0, READERS - 1, first_recv.at[0])

            @pl.when(section > 0)
            def _():
                full(first_0, first_recv.at[0])

        else:
            full(first_in[batch], first_recv.at[batch])
        layer(0, first_in[batch])
        exchange(
            1 + batch, lambda reader: slots_ref[1, reader], second_out.at[batch], section,
            second_in[batch], second_send.at[batch], second_recv.at[batch], True,
        )

    def second(batch):
        arrived(second_in[batch], READERS - 1, second_recv.at[batch])
        layer(1, second_in[batch])

        @pl.when(section < last)
        def _():
            exchange(
                1 + SECTIONS + batch, lambda reader: next_slots[0, reader], first_out.at[batch], section + 1,
                first_in[batch], first_send.at[batch], first_recv.at[batch], False,
            )

        @pl.when(section == last)
        def _():
            for block in range(BLOCKS):
                scaled = held[block].astype(jnp.float32) * (1.0 / CEILING)
                result[batch, :, block * WIDTH : (block + 1) * WIDTH] = scaled.astype(jnp.bfloat16)
            if batch < last:
                pltpu.make_async_remote_copy(
                    src_ref=result.at[batch],
                    dst_ref=landed,
                    send_sem=land_send,
                    recv_sem=land_recv,
                    device_id=(batch, me),
                    device_id_type=MESH,
                ).start()

    first(0)

    @pl.when(section == 0)
    def _():
        pl.semaphore_wait(hello.at[1], 1)
        send_rows(3, start_rows, row_send.at[2], start_row_recv)
        to_table(next_rows, next_slots)

    @pl.when(jnp.logical_and(section > 0, section < last))
    def _():
        full(next_rows, next_row_recv)
        to_table(next_rows, next_slots)

    first(1)
    second(0)
    second(1)
    first(2)
    first(3)
    second(2)
    second(3)

    full(slot_rows, row_send.at[0])

    def gone(index, count, sem):
        arrived(first_0, count, sem)
        full(relay_in.at[index], bundle_send.at[index])
        arrived(first_0, RELAYED, relay_send.at[index])

    direct = READERS - RELAYED

    @pl.when(section == 0)
    def _():
        full(slot_rows, row_send.at[1])
        full(slot_rows, row_send.at[2])
        gone(0, direct - 1, start_send)

    @pl.when(section > 0)
    def _():
        gone(0, direct, start_send)

    for batch in range(SECTIONS):
        gone(1 + batch, direct - 1, second_send.at[batch])

    @pl.when(section < last)
    def _():
        for batch in range(SECTIONS):
            gone(1 + SECTIONS + batch, direct, first_send.at[batch])
        full(landed, land_recv)
        out_ref[...] = landed[...]

    @pl.when(section == last)
    def _():
        full(result.at[pl.ds(0, SECTIONS - 1)], land_send)
        out_ref[...] = result[last]


def per_device(inputs, weights, biases, sources, send_slot):
    slots = send_slot.reshape(2, READERS)
    bf16 = jnp.bfloat16
    pool = (READERS, ROWS, WIDTH)
    grid = (SIDE, SIDE, 2, ROWS, WIDTH)
    rounds = 1 + 2 * SECTIONS
    dma = pltpu.SemaphoreType.DMA
    return pl.pallas_call(
        kernel,
        out_shape=jax.ShapeDtypeStruct((ROWS, BLOCKS * WIDTH), bf16),
        in_specs=[pl.BlockSpec(memory_space=pltpu.HBM)] * 5,
        out_specs=pl.BlockSpec(memory_space=pltpu.VMEM),
        scratch_shapes=[
            pltpu.VMEM((BLOCKS, ROWS, WIDTH), bf16),
            *[pltpu.VMEM(pool, bf16)] * (2 * SECTIONS),
            pltpu.VMEM((SECTIONS, *grid), bf16),
            pltpu.VMEM((SECTIONS, *grid), bf16),
            pltpu.VMEM(grid, bf16),
            pltpu.VMEM(inputs.shape, bf16),
            pltpu.VMEM(weights.shape, bf16),
            pltpu.VMEM(biases.shape, jnp.float32),
            pltpu.SMEM(sources.shape, jnp.int32),
            pltpu.SMEM(slots.shape, jnp.int32),
            pltpu.VMEM(slots.shape, jnp.int32),
            pltpu.VMEM(slots.shape, jnp.int32),
            pltpu.VMEM(slots.shape, jnp.int32),
            pltpu.SMEM(slots.shape, jnp.int32),
            pltpu.SMEM(slots.shape, jnp.int32),
            pltpu.VMEM((SECTIONS, ROWS, BLOCKS * WIDTH), bf16),
            pltpu.VMEM((ROWS, BLOCKS * WIDTH), bf16),
            dma((SECTIONS,)),
            dma((SECTIONS,)),
            dma((SECTIONS,)),
            dma((SECTIONS,)),
            dma(()),
            pltpu.VMEM((rounds, 2, SIDE, ROWS, WIDTH), bf16),
            dma((rounds, 2)),
            dma((rounds,)),
            dma((rounds,)),
            dma((6,)),
            dma((SECTIONS - 1,)),
            dma(()),
            dma(()),
            dma(()),
            dma(()),
            dma(()),
            pltpu.SemaphoreType.REGULAR((2,)),
        ],
        compiler_params=pltpu.CompilerParams(
            collective_id=0, has_side_effects=True, vmem_limit_bytes=60 * 2**20
        ),
        cost_estimate=pl.CostEstimate(flops=2**28, bytes_accessed=2**23, transcendentals=0),
    )(inputs, weights, biases, sources, slots)


def solution(mesh):
    placed = (
        P("segment", "blk"),
        P("segment", "blk", None, None),
        P("segment", "blk"),
        P("segment", "blk", None),
        P("segment", "blk", None, None),
    )
    return jax.shard_map(
        per_device, mesh=mesh, in_specs=placed, out_specs=P("segment", "blk"), check_vma=False
    )
```

```python
import jax
import jax.numpy as jnp
from jax import lax
from jax.experimental import pallas as pl
from jax.experimental.pallas import tpu as pltpu
from jax.sharding import PartitionSpec as P

MESH = pl.DeviceIdType.MESH
CEILING = 32.0
SIDE = 8
READERS = 2 * SIDE * SIDE
SECTIONS = 4
BLOCKS = 4
FAN = 16
ROWS = 8
WIDTH = 128


def kernel(
    inputs_hbm, weights_hbm, biases_hbm, sources_hbm, slots_hbm, out_ref,
    held, first_0, first_1, first_2, first_3, second_0, second_1, second_2, second_3,
    first_out, second_out, start_out, inputs_ref, tiles, biases_ref, sources_ref,
    slots_ref, slot_rows, start_rows, next_rows, start_slots, next_slots, result, landed,
    first_recv, second_recv, first_send, second_send, start_send,
    load_sem, row_send, start_row_recv, next_row_recv, table_sem, land_send, land_recv, hello,
):
    first_in = (first_0, first_1, first_2, first_3)
    second_in = (second_0, second_1, second_2, second_3)
    section = lax.axis_index("segment")
    me = lax.axis_index("blk")
    z, y, core = me // (2 * SIDE), (me // 2) % SIDE, me % 2
    last = SECTIONS - 1
    middle = SIDE // 2

    loads = [
        pltpu.make_async_copy(source, target, load_sem.at[i])
        for i, (source, target) in enumerate((
            (inputs_hbm, inputs_ref),
            (slots_hbm, slots_ref),
            (slots_hbm, slot_rows),
            (sources_hbm, sources_ref),
            (biases_hbm, biases_ref),
            (weights_hbm, tiles),
        ))
    ]
    for load in loads:
        load.start()

    def each_chip(act):
        def chip(dz, dy):
            row = (z + dz + SIDE) % SIDE * SIDE + (y + dy + SIDE) % SIDE
            act(2 * row)
            act(2 * row + 1)

        def some(total, carry):
            total = SIDE - total

            def pair(far_z, inner):
                far_y = total - far_z
                turn_z = jnp.logical_and(far_z > 0, far_z < middle)
                turn_y = jnp.logical_and(far_y > 0, far_y < middle)
                chip(far_z, far_y)

                @pl.when(jnp.logical_and(turn_z, turn_y))
                def _():
                    chip(-far_z, -far_y)

                @pl.when(turn_z)
                def _():
                    chip(-far_z, far_y)

                @pl.when(turn_y)
                def _():
                    chip(far_z, -far_y)

                return inner

            return lax.fori_loop(jnp.maximum(total - middle, 0), jnp.minimum(total, middle) + 1, pair, carry)

        lax.fori_loop(0, SIDE, some, 0)

    barrier = pltpu.get_barrier_semaphore()

    def greet(reader):
        pl.semaphore_signal(barrier, inc=1, device_id=(section, reader), device_id_type=MESH)

    sibling = me + 1 - 2 * core

    @pl.when(section == 0)
    def _():
        for other in range(1, SECTIONS):
            pl.semaphore_signal(barrier, inc=1, device_id=(other, me), device_id_type=MESH)

    @pl.when(jnp.logical_and(section > 0, section < last))
    def _():
        pl.semaphore_signal(barrier, inc=1, device_id=(section + 1, me), device_id_type=MESH)

    each_chip(greet)
    greet(sibling)
    for load in loads[:3]:
        load.wait()
    for block in range(BLOCKS):
        held[block] = inputs_ref[:, block * WIDTH : (block + 1) * WIDTH]
    pl.semaphore_wait(barrier, READERS - 1 + jnp.minimum(section, 2))

    def send_rows(target, arriving, send_sem, recv_sem):
        pltpu.make_async_remote_copy(
            src_ref=slot_rows,
            dst_ref=arriving,
            send_sem=send_sem,
            recv_sem=recv_sem,
            device_id=(target, me),
            device_id_type=MESH,
        ).start()

    def full(ref, sem):
        pltpu.make_async_copy(ref, ref, sem).wait()

    def exchange(slot_of, outgoing, target, arriving, send_sem, recv_sem, own):
        def put(reader):
            outgoing[reader] = held[jnp.minimum(slot_of(reader), BLOCKS - 1)]

        def post(reader):
            put(reader)
            pltpu.make_async_remote_copy(
                src_ref=outgoing.at[reader],
                dst_ref=arriving.at[me],
                send_sem=send_sem,
                recv_sem=recv_sem,
                device_id=(target, reader),
                device_id_type=MESH,
            ).start()

        each_chip(post)
        post(sibling)
        if own:
            arriving[me] = held[jnp.minimum(slot_of(me), BLOCKS - 1)]
        else:
            post(me)

    def arrived(ref, count, sem):
        part = ref.at[pl.ds(0, count)]
        pltpu.make_async_copy(part, part, sem).wait()

    def layer(index, arriving):
        for block in range(BLOCKS):
            parts = [arriving[sources_ref[index, block, k] // BLOCKS] for k in range(FAN)]
            summed = jnp.dot(
                jnp.concatenate(parts, axis=1),
                tiles[index, block],
                preferred_element_type=jnp.float32,
            )
            shifted = summed + biases_ref[index : index + 1, block * WIDTH : (block + 1) * WIDTH]
            held[block] = jnp.clip(shifted, 0.0, CEILING).astype(jnp.bfloat16)

    def to_table(rows, table):
        copy = pltpu.make_async_copy(rows, table, table_sem)
        copy.start()
        copy.wait()


    @pl.when(section == 0)
    def _():
        exchange(
            lambda reader: slots_ref[0, reader],
            start_out, 0, first_0, start_send, first_recv.at[0], True,
        )
        full(next_rows, next_row_recv)
        send_rows(1, start_rows, row_send.at[0], start_row_recv)
        pl.semaphore_wait(hello.at[0], 1)
        send_rows(2, start_rows, row_send.at[1], start_row_recv)

    @pl.when(section > 0)
    def _():
        send_rows(section - 1, next_rows, row_send.at[0], next_row_recv)

    for batch in range(1, SECTIONS):

        @pl.when(section == batch)
        def _():
            if batch > 1:
                pl.semaphore_signal(hello.at[batch - 2], inc=1, device_id=(0, me), device_id_type=MESH)
            full(start_rows, start_row_recv)
            to_table(start_rows, start_slots)
            exchange(
                lambda reader: start_slots[0, reader],
                start_out, 0, first_in[batch], start_send, first_recv.at[batch], False,
            )

    for load in loads[3:]:
        load.wait()

    def first(batch):
        if batch == 0:

            @pl.when(section == 0)
            def _():
                arrived(first_0, READERS - 1, first_recv.at[0])

            @pl.when(section > 0)
            def _():
                full(first_0, first_recv.at[0])

        else:
            full(first_in[batch], first_recv.at[batch])
        layer(0, first_in[batch])
        exchange(
            lambda reader: slots_ref[1, reader], second_out.at[batch], section,
            second_in[batch], second_send.at[batch], second_recv.at[batch], True,
        )

    def second(batch):
        arrived(second_in[batch], READERS - 1, second_recv.at[batch])
        layer(1, second_in[batch])

        @pl.when(section < last)
        def _():
            exchange(
                lambda reader: next_slots[0, reader], first_out.at[batch], section + 1,
                first_in[batch], first_send.at[batch], first_recv.at[batch], False,
            )

        @pl.when(section == last)
        def _():
            for block in range(BLOCKS):
                scaled = held[block].astype(jnp.float32) * (1.0 / CEILING)
                result[batch, :, block * WIDTH : (block + 1) * WIDTH] = scaled.astype(jnp.bfloat16)
            if batch < last:
                pltpu.make_async_remote_copy(
                    src_ref=result.at[batch],
                    dst_ref=landed,
                    send_sem=land_send,
                    recv_sem=land_recv,
                    device_id=(batch, me),
                    device_id_type=MESH,
                ).start()

    first(0)

    @pl.when(section == 0)
    def _():
        pl.semaphore_wait(hello.at[1], 1)
        send_rows(3, start_rows, row_send.at[2], start_row_recv)
        to_table(next_rows, next_slots)

    @pl.when(jnp.logical_and(section > 0, section < last))
    def _():
        full(next_rows, next_row_recv)
        to_table(next_rows, next_slots)

    first(1)
    second(0)
    second(1)
    first(2)
    first(3)
    second(2)
    second(3)

    full(slot_rows, row_send.at[0])

    @pl.when(section == 0)
    def _():
        full(slot_rows, row_send.at[1])
        full(slot_rows, row_send.at[2])
        arrived(start_out, READERS - 1, start_send)

    @pl.when(section > 0)
    def _():
        full(start_out, start_send)

    for batch in range(SECTIONS):
        arrived(second_out.at[batch], READERS - 1, second_send.at[batch])

    @pl.when(section < last)
    def _():
        for batch in range(SECTIONS):
            full(first_out.at[batch], first_send.at[batch])
        full(landed, land_recv)
        out_ref[...] = landed[...]

    @pl.when(section == last)
    def _():
        full(result.at[pl.ds(0, SECTIONS - 1)], land_send)
        out_ref[...] = result[last]


def per_device(inputs, weights, biases, sources, send_slot):
    slots = send_slot.reshape(2, READERS)
    bf16 = jnp.bfloat16
    pool = (READERS, ROWS, WIDTH)
    dma = pltpu.SemaphoreType.DMA
    return pl.pallas_call(
        kernel,
        out_shape=jax.ShapeDtypeStruct((ROWS, BLOCKS * WIDTH), bf16),
        in_specs=[pl.BlockSpec(memory_space=pltpu.HBM)] * 5,
        out_specs=pl.BlockSpec(memory_space=pltpu.VMEM),
        scratch_shapes=[
            pltpu.VMEM((BLOCKS, ROWS, WIDTH), bf16),
            *[pltpu.VMEM(pool, bf16)] * (2 * SECTIONS),
            pltpu.VMEM((SECTIONS, *pool), bf16),
            pltpu.VMEM((SECTIONS, *pool), bf16),
            pltpu.VMEM(pool, bf16),
            pltpu.VMEM(inputs.shape, bf16),
            pltpu.VMEM(weights.shape, bf16),
            pltpu.VMEM(biases.shape, jnp.float32),
            pltpu.SMEM(sources.shape, jnp.int32),
            pltpu.SMEM(slots.shape, jnp.int32),
            pltpu.VMEM(slots.shape, jnp.int32),
            pltpu.VMEM(slots.shape, jnp.int32),
            pltpu.VMEM(slots.shape, jnp.int32),
            pltpu.SMEM(slots.shape, jnp.int32),
            pltpu.SMEM(slots.shape, jnp.int32),
            pltpu.VMEM((SECTIONS, ROWS, BLOCKS * WIDTH), bf16),
            pltpu.VMEM((ROWS, BLOCKS * WIDTH), bf16),
            dma((SECTIONS,)),
            dma((SECTIONS,)),
            dma((SECTIONS,)),
            dma((SECTIONS,)),
            dma(()),
            dma((6,)),
            dma((SECTIONS - 1,)),
            dma(()),
            dma(()),
            dma(()),
            dma(()),
            dma(()),
            pltpu.SemaphoreType.REGULAR((2,)),
        ],
        compiler_params=pltpu.CompilerParams(
            collective_id=0, has_side_effects=True, vmem_limit_bytes=60 * 2**20
        ),
        cost_estimate=pl.CostEstimate(flops=2**28, bytes_accessed=2**23, transcendentals=0),
    )(inputs, weights, biases, sources, slots)


def solution(mesh):
    placed = (
        P("segment", "blk"),
        P("segment", "blk", None, None),
        P("segment", "blk"),
        P("segment", "blk", None),
        P("segment", "blk", None, None),
    )
    return jax.shard_map(
        per_device, mesh=mesh, in_specs=placed, out_specs=P("segment", "blk"), check_vma=False
    )
```

```python
import jax
import jax.numpy as jnp
from jax import lax
from jax.experimental import pallas as pl
from jax.experimental.pallas import tpu as pltpu
from jax.sharding import PartitionSpec as P

MESH = pl.DeviceIdType.MESH
CEILING = 32.0
SIDE = 8
READERS = 2 * SIDE * SIDE
SECTIONS = 4
BLOCKS = 4
FAN = 16
ROWS = 8
WIDTH = 128
PASSED = 2


def kernel(
    inputs_hbm, weights_hbm, biases_hbm, sources_hbm, slots_hbm, out_ref,
    held, first_0, first_1, first_2, first_3, second_0, second_1, second_2, second_3,
    passed_0, passed_1, passed_out, pass_send, pass_recv,
    first_out, second_out, start_out, inputs_ref, tiles, biases_ref, sources_ref,
    slots_ref, slot_rows, start_rows, next_rows, start_slots, next_slots, result, landed,
    first_recv, second_recv, first_send, second_send, start_send,
    load_sem, row_send, start_row_recv, next_row_recv, table_sem, land_send, land_recv, hello,
):
    first_in = (first_0, first_1, first_2, first_3)
    second_in = (second_0, second_1, second_2, second_3)
    passed_in = (passed_0, passed_1)
    section = lax.axis_index("segment")
    me = lax.axis_index("blk")
    z, y, core = me // (2 * SIDE), (me // 2) % SIDE, me % 2
    last = SECTIONS - 1
    middle = SIDE // 2

    loads = [
        pltpu.make_async_copy(source, target, load_sem.at[i])
        for i, (source, target) in enumerate((
            (inputs_hbm, inputs_ref),
            (slots_hbm, slots_ref),
            (slots_hbm, slot_rows),
            (sources_hbm, sources_ref),
            (biases_hbm, biases_ref),
            (weights_hbm, tiles),
        ))
    ]
    for load in loads:
        load.start()

    def each_chip(act):
        def chip(dz, dy):
            row = (z + dz + SIDE) % SIDE * SIDE + (y + dy + SIDE) % SIDE
            act(2 * row)
            act(2 * row + 1)

        def some(total, carry):
            total = SIDE - total

            def pair(far_z, inner):
                far_y = total - far_z
                turn_z = jnp.logical_and(far_z > 0, far_z < middle)
                turn_y = jnp.logical_and(far_y > 0, far_y < middle)
                chip(far_z, far_y)

                @pl.when(jnp.logical_and(turn_z, turn_y))
                def _():
                    chip(-far_z, -far_y)

                @pl.when(turn_z)
                def _():
                    chip(-far_z, far_y)

                @pl.when(turn_y)
                def _():
                    chip(far_z, -far_y)

                return inner

            return lax.fori_loop(jnp.maximum(total - middle, 0), jnp.minimum(total, middle) + 1, pair, carry)

        lax.fori_loop(0, SIDE, some, 0)

    barrier = pltpu.get_barrier_semaphore()

    def greet(reader):
        pl.semaphore_signal(barrier, inc=1, device_id=(section, reader), device_id_type=MESH)

    sibling = me + 1 - 2 * core

    @pl.when(section == 0)
    def _():
        for other in range(1, SECTIONS):
            pl.semaphore_signal(barrier, inc=1, device_id=(other, me), device_id_type=MESH)

    @pl.when(jnp.logical_and(section > 0, section < last))
    def _():
        pl.semaphore_signal(barrier, inc=1, device_id=(section + 1, me), device_id_type=MESH)

    each_chip(greet)
    greet(sibling)
    for load in loads[:3]:
        load.wait()
    for block in range(BLOCKS):
        held[block] = inputs_ref[:, block * WIDTH : (block + 1) * WIDTH]
    pl.semaphore_wait(barrier, READERS - 1 + jnp.minimum(section, 2))

    def send_rows(target, arriving, send_sem, recv_sem):
        pltpu.make_async_remote_copy(
            src_ref=slot_rows,
            dst_ref=arriving,
            send_sem=send_sem,
            recv_sem=recv_sem,
            device_id=(target, me),
            device_id_type=MESH,
        ).start()

    def full(ref, sem):
        pltpu.make_async_copy(ref, ref, sem).wait()

    def exchange(blocks, slot_of, outgoing, target, arriving, send_sem, recv_sem, own):
        def put(reader):
            outgoing[reader] = blocks[jnp.minimum(slot_of(reader), BLOCKS - 1)]

        def post(reader):
            put(reader)
            pltpu.make_async_remote_copy(
                src_ref=outgoing.at[reader],
                dst_ref=arriving.at[me],
                send_sem=send_sem,
                recv_sem=recv_sem,
                device_id=(target, reader),
                device_id_type=MESH,
            ).start()

        each_chip(post)
        post(sibling)
        if own:
            arriving[me] = blocks[jnp.minimum(slot_of(me), BLOCKS - 1)]
        else:
            post(me)

    def arrived(ref, count, sem):
        part = ref.at[pl.ds(0, count)]
        pltpu.make_async_copy(part, part, sem).wait()

    def layer(index, arriving):
        for block in range(BLOCKS):
            parts = [arriving[sources_ref[index, block, k] // BLOCKS] for k in range(FAN)]
            summed = jnp.dot(
                jnp.concatenate(parts, axis=1),
                tiles[index, block],
                preferred_element_type=jnp.float32,
            )
            shifted = summed + biases_ref[index : index + 1, block * WIDTH : (block + 1) * WIDTH]
            held[block] = jnp.clip(shifted, 0.0, CEILING).astype(jnp.bfloat16)

    def to_table(rows, table):
        copy = pltpu.make_async_copy(rows, table, table_sem)
        copy.start()
        copy.wait()


    @pl.when(section == 0)
    def _():
        exchange(
            held, lambda reader: slots_ref[0, reader],
            start_out, 0, first_0, start_send, first_recv.at[0], True,
        )
        full(next_rows, next_row_recv)
        send_rows(1, start_rows, row_send.at[0], start_row_recv)
        pl.semaphore_wait(hello.at[0], 1)
        send_rows(2, start_rows, row_send.at[1], start_row_recv)

    @pl.when(section > 0)
    def _():
        send_rows(section - 1, next_rows, row_send.at[0], next_row_recv)

    for batch in range(1, SECTIONS):

        @pl.when(section == batch)
        def _():
            if batch > 1:
                pl.semaphore_signal(hello.at[batch - 2], inc=1, device_id=(0, me), device_id_type=MESH)
            full(start_rows, start_row_recv)
            to_table(start_rows, start_slots)
            exchange(
                held, lambda reader: start_slots[0, reader],
                start_out, 0, first_in[batch], start_send, first_recv.at[batch], False,
            )

    for load in loads[3:]:
        load.wait()

    def first(batch):
        if batch == 0:
            arrived(first_0, READERS - 1, first_recv.at[0])
        elif batch < PASSED:

            @pl.when(section == 0)
            def _():
                full(first_in[batch], first_recv.at[batch])

            @pl.when(section > 0)
            def _():
                arrived(first_in[batch], READERS - 1, first_recv.at[batch])

        else:
            full(first_in[batch], first_recv.at[batch])
        layer(0, first_in[batch])
        exchange(
            held, lambda reader: slots_ref[1, reader], second_out.at[batch], section,
            second_in[batch], second_send.at[batch], second_recv.at[batch], True,
        )

    def second(batch):
        arrived(second_in[batch], READERS - 1, second_recv.at[batch])
        layer(1, second_in[batch])

        @pl.when(section < last)
        def _():
            if batch < PASSED:
                passed_out[batch] = held[...]
                pltpu.make_async_remote_copy(
                    src_ref=passed_out.at[batch],
                    dst_ref=passed_in[batch],
                    send_sem=pass_send.at[batch],
                    recv_sem=pass_recv.at[batch],
                    device_id=(section + 1, me),
                    device_id_type=MESH,
                ).start()
            else:
                exchange(
                    held, lambda reader: next_slots[0, reader], first_out.at[batch], section + 1,
                    first_in[batch], first_send.at[batch], first_recv.at[batch], False,
                )

        @pl.when(section == last)
        def _():
            for block in range(BLOCKS):
                scaled = held[block].astype(jnp.float32) * (1.0 / CEILING)
                result[batch, :, block * WIDTH : (block + 1) * WIDTH] = scaled.astype(jnp.bfloat16)
            if batch < last:
                pltpu.make_async_remote_copy(
                    src_ref=result.at[batch],
                    dst_ref=landed,
                    send_sem=land_send,
                    recv_sem=land_recv,
                    device_id=(batch, me),
                    device_id_type=MESH,
                ).start()

    @pl.when(section > 0)
    def _():
        for batch in range(PASSED):
            full(passed_in[batch], pass_recv.at[batch])
            exchange(
                passed_in[batch], lambda reader: slots_ref[0, reader], first_out.at[batch], section,
                first_in[batch], first_send.at[batch], first_recv.at[batch], True,
            )

    first(0)

    @pl.when(section == 0)
    def _():
        pl.semaphore_wait(hello.at[1], 1)
        send_rows(3, start_rows, row_send.at[2], start_row_recv)
        to_table(next_rows, next_slots)

    @pl.when(jnp.logical_and(section > 0, section < last))
    def _():
        full(next_rows, next_row_recv)
        to_table(next_rows, next_slots)

    first(1)
    second(0)
    first(2)
    second(1)
    first(3)
    second(2)
    second(3)

    full(slot_rows, row_send.at[0])

    @pl.when(section == 0)
    def _():
        full(slot_rows, row_send.at[1])
        full(slot_rows, row_send.at[2])
        arrived(start_out, READERS - 1, start_send)

    @pl.when(section > 0)
    def _():
        full(start_out, start_send)
        for batch in range(PASSED):
            arrived(first_out.at[batch], READERS - 1, first_send.at[batch])

    for batch in range(SECTIONS):
        arrived(second_out.at[batch], READERS - 1, second_send.at[batch])

    @pl.when(section < last)
    def _():
        for batch in range(SECTIONS):
            if batch < PASSED:
                full(passed_out.at[batch], pass_send.at[batch])
            else:
                full(first_out.at[batch], first_send.at[batch])
        full(landed, land_recv)
        out_ref[...] = landed[...]

    @pl.when(section == last)
    def _():
        full(result.at[pl.ds(0, SECTIONS - 1)], land_send)
        out_ref[...] = result[last]


def per_device(inputs, weights, biases, sources, send_slot):
    slots = send_slot.reshape(2, READERS)
    bf16 = jnp.bfloat16
    pool = (READERS, ROWS, WIDTH)
    dma = pltpu.SemaphoreType.DMA
    return pl.pallas_call(
        kernel,
        out_shape=jax.ShapeDtypeStruct((ROWS, BLOCKS * WIDTH), bf16),
        in_specs=[pl.BlockSpec(memory_space=pltpu.HBM)] * 5,
        out_specs=pl.BlockSpec(memory_space=pltpu.VMEM),
        scratch_shapes=[
            pltpu.VMEM((BLOCKS, ROWS, WIDTH), bf16),
            *[pltpu.VMEM(pool, bf16)] * (2 * SECTIONS),
            *[pltpu.VMEM((BLOCKS, ROWS, WIDTH), bf16)] * PASSED,
            pltpu.VMEM((PASSED, BLOCKS, ROWS, WIDTH), bf16),
            dma((PASSED,)),
            dma((PASSED,)),
            pltpu.VMEM((SECTIONS, *pool), bf16),
            pltpu.VMEM((SECTIONS, *pool), bf16),
            pltpu.VMEM(pool, bf16),
            pltpu.VMEM(inputs.shape, bf16),
            pltpu.VMEM(weights.shape, bf16),
            pltpu.VMEM(biases.shape, jnp.float32),
            pltpu.SMEM(sources.shape, jnp.int32),
            pltpu.SMEM(slots.shape, jnp.int32),
            pltpu.VMEM(slots.shape, jnp.int32),
            pltpu.VMEM(slots.shape, jnp.int32),
            pltpu.VMEM(slots.shape, jnp.int32),
            pltpu.SMEM(slots.shape, jnp.int32),
            pltpu.SMEM(slots.shape, jnp.int32),
            pltpu.VMEM((SECTIONS, ROWS, BLOCKS * WIDTH), bf16),
            pltpu.VMEM((ROWS, BLOCKS * WIDTH), bf16),
            dma((SECTIONS,)),
            dma((SECTIONS,)),
            dma((SECTIONS,)),
            dma((SECTIONS,)),
            dma(()),
            dma((6,)),
            dma((SECTIONS - 1,)),
            dma(()),
            dma(()),
            dma(()),
            dma(()),
            dma(()),
            pltpu.SemaphoreType.REGULAR((2,)),
        ],
        compiler_params=pltpu.CompilerParams(
            collective_id=0, has_side_effects=True, vmem_limit_bytes=60 * 2**20
        ),
        cost_estimate=pl.CostEstimate(flops=2**28, bytes_accessed=2**23, transcendentals=0),
    )(inputs, weights, biases, sources, slots)


def solution(mesh):
    placed = (
        P("segment", "blk"),
        P("segment", "blk", None, None),
        P("segment", "blk"),
        P("segment", "blk", None),
        P("segment", "blk", None, None),
    )
    return jax.shard_map(
        per_device, mesh=mesh, in_specs=placed, out_specs=P("segment", "blk"), check_vma=False
    )
```

```python
import jax
import jax.numpy as jnp
from jax import lax
from jax.experimental import pallas as pl
from jax.experimental.pallas import tpu as pltpu
from jax.sharding import PartitionSpec as P

MESH = pl.DeviceIdType.MESH
CEILING = 32.0
SIDE = 8
READERS = 2 * SIDE * SIDE
SECTIONS = 4
BLOCKS = 4
FAN = 16
ROWS = 8
WIDTH = 128
PASSES = ((0, 1, 2), (0, 2))
PASSED = len(PASSES)
LENT = ((1, 2), (1, 3), (3, 2))


def kernel(
    inputs_hbm, weights_hbm, biases_hbm, sources_hbm, slots_hbm, out_ref,
    held, first_0, first_1, first_2, first_3, second_0, second_1, second_2, second_3,
    passed_0, passed_1, passed_out, pass_send, pass_recv, passed_pool, passed_pool_send,
    lent_0, lent_1, lent_2, lent_out, lent_pool, lent_send, lent_recv, lent_pool_send,
    end_rows, end_row_recv, end_slots,
    first_out, second_out, start_out, inputs_ref, tiles, biases_ref, sources_ref,
    slots_ref, slot_rows, start_rows, next_rows, start_slots, next_slots, result, landed,
    first_recv, second_recv, first_send, second_send, start_send,
    load_sem, row_send, start_row_recv, next_row_recv, table_sem, land_send, land_recv, hello,
):
    first_in = (first_0, first_1, first_2, first_3)
    second_in = (second_0, second_1, second_2, second_3)
    passed_in = (passed_0, passed_1)
    lent_in = (lent_0, lent_1, lent_2)
    section = lax.axis_index("segment")
    me = lax.axis_index("blk")
    z, y, core = me // (2 * SIDE), (me // 2) % SIDE, me % 2
    last = SECTIONS - 1

    def is_one_of(sections):
        found = section < 0
        for one in sections:
            found = jnp.logical_or(found, section == one)
        return found

    def lenders(batch):
        return [lender for lender, lent in LENT if lent == batch]

    middle = SIDE // 2

    loads = [
        pltpu.make_async_copy(source, target, load_sem.at[i])
        for i, (source, target) in enumerate((
            (inputs_hbm, inputs_ref),
            (slots_hbm, slots_ref),
            (slots_hbm, slot_rows),
            (sources_hbm, sources_ref),
            (biases_hbm, biases_ref),
            (weights_hbm, tiles),
        ))
    ]
    for load in loads:
        load.start()

    def each_chip(act):
        def chip(dz, dy):
            row = (z + dz + SIDE) % SIDE * SIDE + (y + dy + SIDE) % SIDE
            act(2 * row)
            act(2 * row + 1)

        def some(total, carry):
            total = SIDE - total

            def pair(far_z, inner):
                far_y = total - far_z
                turn_z = jnp.logical_and(far_z > 0, far_z < middle)
                turn_y = jnp.logical_and(far_y > 0, far_y < middle)
                chip(far_z, far_y)

                @pl.when(jnp.logical_and(turn_z, turn_y))
                def _():
                    chip(-far_z, -far_y)

                @pl.when(turn_z)
                def _():
                    chip(-far_z, far_y)

                @pl.when(turn_y)
                def _():
                    chip(far_z, -far_y)

                return inner

            return lax.fori_loop(jnp.maximum(total - middle, 0), jnp.minimum(total, middle) + 1, pair, carry)

        lax.fori_loop(0, SIDE, some, 0)

    barrier = pltpu.get_barrier_semaphore()

    def greet(reader):
        pl.semaphore_signal(barrier, inc=1, device_id=(section, reader), device_id_type=MESH)

    sibling = me + 1 - 2 * core

    @pl.when(section == 0)
    def _():
        for other in range(1, SECTIONS):
            pl.semaphore_signal(barrier, inc=1, device_id=(other, me), device_id_type=MESH)

    @pl.when(jnp.logical_and(section > 0, section < last))
    def _():
        pl.semaphore_signal(barrier, inc=1, device_id=(section + 1, me), device_id_type=MESH)

    each_chip(greet)
    greet(sibling)
    for load in loads[:3]:
        load.wait()
    for block in range(BLOCKS):
        held[block] = inputs_ref[:, block * WIDTH : (block + 1) * WIDTH]
    pl.semaphore_wait(barrier, READERS - 1 + jnp.minimum(section, 2))

    def send_rows(target, arriving, send_sem, recv_sem):
        pltpu.make_async_remote_copy(
            src_ref=slot_rows,
            dst_ref=arriving,
            send_sem=send_sem,
            recv_sem=recv_sem,
            device_id=(target, me),
            device_id_type=MESH,
        ).start()

    def full(ref, sem):
        pltpu.make_async_copy(ref, ref, sem).wait()

    def exchange(blocks, slot_of, outgoing, target, arriving, send_sem, recv_sem, own):
        def put(reader):
            outgoing[reader] = blocks[jnp.minimum(slot_of(reader), BLOCKS - 1)]

        def post(reader):
            put(reader)
            pltpu.make_async_remote_copy(
                src_ref=outgoing.at[reader],
                dst_ref=arriving.at[me],
                send_sem=send_sem,
                recv_sem=recv_sem,
                device_id=(target, reader),
                device_id_type=MESH,
            ).start()

        each_chip(post)
        post(sibling)
        if own:
            arriving[me] = blocks[jnp.minimum(slot_of(me), BLOCKS - 1)]
        else:
            post(me)

    def arrived(ref, count, sem):
        part = ref.at[pl.ds(0, count)]
        pltpu.make_async_copy(part, part, sem).wait()

    def layer(index, arriving):
        for block in range(BLOCKS):
            parts = [arriving[sources_ref[index, block, k] // BLOCKS] for k in range(FAN)]
            summed = jnp.dot(
                jnp.concatenate(parts, axis=1),
                tiles[index, block],
                preferred_element_type=jnp.float32,
            )
            shifted = summed + biases_ref[index : index + 1, block * WIDTH : (block + 1) * WIDTH]
            held[block] = jnp.clip(shifted, 0.0, CEILING).astype(jnp.bfloat16)

    def to_table(rows, table):
        copy = pltpu.make_async_copy(rows, table, table_sem)
        copy.start()
        copy.wait()


    @pl.when(section == 0)
    def _():
        exchange(
            held, lambda reader: slots_ref[0, reader],
            start_out, 0, first_0, start_send, first_recv.at[0], True,
        )
        full(next_rows, next_row_recv)
        send_rows(1, start_rows, row_send.at[0], start_row_recv)
        pl.semaphore_wait(hello.at[0], 1)
        send_rows(2, start_rows, row_send.at[1], start_row_recv)

    @pl.when(section > 0)
    def _():
        send_rows(section - 1, next_rows, row_send.at[0], next_row_recv)

    @pl.when(section == last)
    def _():
        send_rows(0, end_rows, row_send.at[1], end_row_recv)

    for batch in range(1, SECTIONS):

        @pl.when(section == batch)
        def _():
            if batch > 1:
                pl.semaphore_signal(hello.at[batch - 2], inc=1, device_id=(0, me), device_id_type=MESH)
            full(start_rows, start_row_recv)
            to_table(start_rows, start_slots)
            exchange(
                held, lambda reader: start_slots[0, reader],
                start_out, 0, first_in[batch], start_send, first_recv.at[batch], False,
            )

    for load in loads[3:]:
        load.wait()

    def landed_pool(ref, inside, sem):
        @pl.when(inside)
        def _():
            arrived(ref, READERS - 1, sem)

        @pl.when(jnp.logical_not(inside))
        def _():
            full(ref, sem)

    def passes(batch, back):
        return is_one_of([one + back for one in PASSES[batch]]) if batch < PASSED else section < 0

    def first(batch):
        inside = passes(batch, 1)
        if batch == 0:
            inside = jnp.logical_or(inside, section == 0)
        landed_pool(first_in[batch], inside, first_recv.at[batch])
        layer(0, first_in[batch])

        @pl.when(jnp.logical_not(is_one_of(lenders(batch))))
        def _():
            exchange(
                held, lambda reader: slots_ref[1, reader], second_out.at[batch], section,
                second_in[batch], second_send.at[batch], second_recv.at[batch], True,
            )

        for i, (lender, lent) in enumerate(LENT):
            if lent == batch:

                @pl.when(section == lender)
                def _():
                    lent_out[i] = held[...]
                    pltpu.make_async_remote_copy(
                        src_ref=lent_out.at[i],
                        dst_ref=lent_in[i],
                        send_sem=lent_send.at[i],
                        recv_sem=lent_recv.at[i],
                        device_id=(0, me),
                        device_id_type=MESH,
                    ).start()

    def second(batch):
        landed_pool(second_in[batch], jnp.logical_not(is_one_of(lenders(batch))), second_recv.at[batch])
        layer(1, second_in[batch])

        if batch < PASSED:

            @pl.when(passes(batch, 0))
            def _():
                passed_out[batch] = held[...]
                pltpu.make_async_remote_copy(
                    src_ref=passed_out.at[batch],
                    dst_ref=passed_in[batch],
                    send_sem=pass_send.at[batch],
                    recv_sem=pass_recv.at[batch],
                    device_id=(section + 1, me),
                    device_id_type=MESH,
                ).start()

        @pl.when(jnp.logical_and(section < last, jnp.logical_not(passes(batch, 0))))
        def _():
            exchange(
                held, lambda reader: next_slots[0, reader], first_out.at[batch], section + 1,
                first_in[batch], first_send.at[batch], first_recv.at[batch], False,
            )

        @pl.when(section == last)
        def _():
            for block in range(BLOCKS):
                scaled = held[block].astype(jnp.float32) * (1.0 / CEILING)
                result[batch, :, block * WIDTH : (block + 1) * WIDTH] = scaled.astype(jnp.bfloat16)
            if batch < last:
                pltpu.make_async_remote_copy(
                    src_ref=result.at[batch],
                    dst_ref=landed,
                    send_sem=land_send,
                    recv_sem=land_recv,
                    device_id=(batch, me),
                    device_id_type=MESH,
                ).start()

    for batch in range(PASSED):

        @pl.when(passes(batch, 1))
        def _():
            full(passed_in[batch], pass_recv.at[batch])
            exchange(
                passed_in[batch], lambda reader: slots_ref[0, reader], passed_pool.at[batch], section,
                first_in[batch], passed_pool_send.at[batch], first_recv.at[batch], True,
            )

    first(0)

    @pl.when(section == 0)
    def _():
        pl.semaphore_wait(hello.at[1], 1)
        send_rows(3, start_rows, row_send.at[2], start_row_recv)
        to_table(next_rows, next_slots)

    @pl.when(jnp.logical_and(section > 0, section < last))
    def _():
        full(next_rows, next_row_recv)
        to_table(next_rows, next_slots)

    first(1)
    second(0)
    first(2)
    second(1)
    first(3)
    second(2)
    second(3)

    @pl.when(section == 0)
    def _():
        full(end_rows, end_row_recv)
        to_table(end_rows, end_slots)
        for i, (lender, batch) in enumerate(LENT):
            table = next_slots if lender == 1 else end_slots
            full(lent_in[i], lent_recv.at[i])
            exchange(
                lent_in[i], lambda reader: table[1, reader], lent_pool.at[i], lender,
                second_in[batch], lent_pool_send.at[i], second_recv.at[batch], False,
            )
        for i in range(len(LENT)):
            full(lent_pool.at[i], lent_pool_send.at[i])

    for i, (lender, _) in enumerate(LENT):

        @pl.when(section == lender)
        def _():
            full(lent_out.at[i], lent_send.at[i])

    @pl.when(section == last)
    def _():
        full(slot_rows, row_send.at[1])

    full(slot_rows, row_send.at[0])

    @pl.when(section == 0)
    def _():
        full(slot_rows, row_send.at[1])
        full(slot_rows, row_send.at[2])
        arrived(start_out, READERS - 1, start_send)

    @pl.when(section > 0)
    def _():
        full(start_out, start_send)

    for batch in range(SECTIONS):

        @pl.when(jnp.logical_not(is_one_of(lenders(batch))))
        def _():
            arrived(second_out.at[batch], READERS - 1, second_send.at[batch])

        if batch < PASSED:

            @pl.when(passes(batch, 0))
            def _():
                full(passed_out.at[batch], pass_send.at[batch])

            @pl.when(passes(batch, 1))
            def _():
                arrived(passed_pool.at[batch], READERS - 1, passed_pool_send.at[batch])

        @pl.when(jnp.logical_and(section < last, jnp.logical_not(passes(batch, 0))))
        def _():
            full(first_out.at[batch], first_send.at[batch])

    @pl.when(section < last)
    def _():
        full(landed, land_recv)
        out_ref[...] = landed[...]

    @pl.when(section == last)
    def _():
        full(result.at[pl.ds(0, SECTIONS - 1)], land_send)
        out_ref[...] = result[last]


def per_device(inputs, weights, biases, sources, send_slot):
    slots = send_slot.reshape(2, READERS)
    bf16 = jnp.bfloat16
    pool = (READERS, ROWS, WIDTH)
    dma = pltpu.SemaphoreType.DMA
    return pl.pallas_call(
        kernel,
        out_shape=jax.ShapeDtypeStruct((ROWS, BLOCKS * WIDTH), bf16),
        in_specs=[pl.BlockSpec(memory_space=pltpu.HBM)] * 5,
        out_specs=pl.BlockSpec(memory_space=pltpu.VMEM),
        scratch_shapes=[
            pltpu.VMEM((BLOCKS, ROWS, WIDTH), bf16),
            *[pltpu.VMEM(pool, bf16)] * (2 * SECTIONS),
            *[pltpu.VMEM((BLOCKS, ROWS, WIDTH), bf16)] * PASSED,
            pltpu.VMEM((PASSED, BLOCKS, ROWS, WIDTH), bf16),
            dma((PASSED,)),
            dma((PASSED,)),
            pltpu.VMEM((PASSED, *pool), bf16),
            dma((PASSED,)),
            *[pltpu.VMEM((BLOCKS, ROWS, WIDTH), bf16)] * len(LENT),
            pltpu.VMEM((len(LENT), BLOCKS, ROWS, WIDTH), bf16),
            pltpu.VMEM((len(LENT), *pool), bf16),
            dma((len(LENT),)),
            dma((len(LENT),)),
            dma((len(LENT),)),
            pltpu.VMEM(slots.shape, jnp.int32),
            dma(()),
            pltpu.SMEM(slots.shape, jnp.int32),
            pltpu.VMEM((SECTIONS, *pool), bf16),
            pltpu.VMEM((SECTIONS, *pool), bf16),
            pltpu.VMEM(pool, bf16),
            pltpu.VMEM(inputs.shape, bf16),
            pltpu.VMEM(weights.shape, bf16),
            pltpu.VMEM(biases.shape, jnp.float32),
            pltpu.SMEM(sources.shape, jnp.int32),
            pltpu.SMEM(slots.shape, jnp.int32),
            pltpu.VMEM(slots.shape, jnp.int32),
            pltpu.VMEM(slots.shape, jnp.int32),
            pltpu.VMEM(slots.shape, jnp.int32),
            pltpu.SMEM(slots.shape, jnp.int32),
            pltpu.SMEM(slots.shape, jnp.int32),
            pltpu.VMEM((SECTIONS, ROWS, BLOCKS * WIDTH), bf16),
            pltpu.VMEM((ROWS, BLOCKS * WIDTH), bf16),
            dma((SECTIONS,)),
            dma((SECTIONS,)),
            dma((SECTIONS,)),
            dma((SECTIONS,)),
            dma(()),
            dma((6,)),
            dma((SECTIONS - 1,)),
            dma(()),
            dma(()),
            dma(()),
            dma(()),
            dma(()),
            pltpu.SemaphoreType.REGULAR((2,)),
        ],
        compiler_params=pltpu.CompilerParams(
            collective_id=0, has_side_effects=True, vmem_limit_bytes=60 * 2**20
        ),
        cost_estimate=pl.CostEstimate(flops=2**28, bytes_accessed=2**23, transcendentals=0),
    )(inputs, weights, biases, sources, slots)


def solution(mesh):
    placed = (
        P("segment", "blk"),
        P("segment", "blk", None, None),
        P("segment", "blk"),
        P("segment", "blk", None),
        P("segment", "blk", None, None),
    )
    return jax.shard_map(
        per_device, mesh=mesh, in_specs=placed, out_specs=P("segment", "blk"), check_vma=False
    )
```

```python
import jax
import jax.numpy as jnp
from jax import lax
from jax.experimental import pallas as pl
from jax.experimental.pallas import tpu as pltpu
from jax.sharding import PartitionSpec as P

MESH = pl.DeviceIdType.MESH
CEILING = 32.0
SIDE = 8
READERS = 2 * SIDE * SIDE
SECTIONS = 4
BLOCKS = 4
FAN = 16
ROWS = 8
WIDTH = 128
PASSED = 2


def chips_by_distance():
    half = range(SIDE // 2 + 1)
    found = []
    for far_z, far_y in sorted(((a, b) for a in half for b in half), key=lambda far: -sum(far)):
        for dz, dy in ((far_z, far_y), (-far_z, -far_y), (-far_z, far_y), (far_z, -far_y)):
            offset = (dz % SIDE, dy % SIDE)
            if offset not in found and offset != (0, 0):
                found.append(offset)
    return found


def kernel(
    inputs_hbm, weights_hbm, biases_hbm, sources_hbm, slots_hbm, out_ref,
    held, first_0, first_1, first_2, first_3, second_0, second_1, second_2, second_3,
    passed_0, passed_1, passed_out, pass_send, pass_recv,
    first_out, second_out, start_out, inputs_ref, tiles, biases_ref, sources_ref,
    slots_ref, slot_rows, start_rows, next_rows, start_slots, next_slots, result, landed,
    first_recv, second_recv, first_send, second_send, start_send,
    load_sem, row_send, start_row_recv, next_row_recv, table_sem, land_send, land_recv, hello,
):
    first_in = (first_0, first_1, first_2, first_3)
    second_in = (second_0, second_1, second_2, second_3)
    passed_in = (passed_0, passed_1)
    section = lax.axis_index("segment")
    me = lax.axis_index("blk")
    z, y, core = me // (2 * SIDE), (me // 2) % SIDE, me % 2
    last = SECTIONS - 1
    middle = SIDE // 2

    loads = [
        pltpu.make_async_copy(source, target, load_sem.at[i])
        for i, (source, target) in enumerate((
            (inputs_hbm, inputs_ref),
            (slots_hbm, slots_ref),
            (slots_hbm, slot_rows),
            (sources_hbm, sources_ref),
            (biases_hbm, biases_ref),
            (weights_hbm, tiles),
        ))
    ]
    for load in loads:
        load.start()

    rows = [(z + step) % SIDE * SIDE for step in range(SIDE)]
    columns = [(y + step) % SIDE for step in range(SIDE)]

    def each_chip(act):
        for dz, dy in chips_by_distance():
            chip = rows[dz] + columns[dy]
            act(2 * chip)
            act(2 * chip + 1)

    barrier = pltpu.get_barrier_semaphore()

    def greet(reader):
        pl.semaphore_signal(barrier, inc=1, device_id=(section, reader), device_id_type=MESH)

    sibling = me + 1 - 2 * core

    @pl.when(section == 0)
    def _():
        for other in range(1, SECTIONS):
            pl.semaphore_signal(barrier, inc=1, device_id=(other, me), device_id_type=MESH)

    @pl.when(jnp.logical_and(section > 0, section < last))
    def _():
        pl.semaphore_signal(barrier, inc=1, device_id=(section + 1, me), device_id_type=MESH)

    each_chip(greet)
    greet(sibling)
    for load in loads[:3]:
        load.wait()
    for block in range(BLOCKS):
        held[block] = inputs_ref[:, block * WIDTH : (block + 1) * WIDTH]
    pl.semaphore_wait(barrier, READERS - 1 + jnp.minimum(section, 2))

    def send_rows(target, arriving, send_sem, recv_sem):
        pltpu.make_async_remote_copy(
            src_ref=slot_rows,
            dst_ref=arriving,
            send_sem=send_sem,
            recv_sem=recv_sem,
            device_id=(target, me),
            device_id_type=MESH,
        ).start()

    def full(ref, sem):
        pltpu.make_async_copy(ref, ref, sem).wait()

    def exchange(blocks, slot_of, outgoing, target, arriving, send_sem, recv_sem, own):
        def put(reader):
            outgoing[reader] = blocks[jnp.minimum(slot_of(reader), BLOCKS - 1)]

        def post(reader):
            put(reader)
            pltpu.make_async_remote_copy(
                src_ref=outgoing.at[reader],
                dst_ref=arriving.at[me],
                send_sem=send_sem,
                recv_sem=recv_sem,
                device_id=(target, reader),
                device_id_type=MESH,
            ).start()

        each_chip(post)
        post(sibling)
        if own:
            arriving[me] = blocks[jnp.minimum(slot_of(me), BLOCKS - 1)]
        else:
            post(me)

    def arrived(ref, count, sem):
        part = ref.at[pl.ds(0, count)]
        pltpu.make_async_copy(part, part, sem).wait()

    def layer(index, arriving):
        for block in range(BLOCKS):
            parts = [arriving[sources_ref[index, block, k] // BLOCKS] for k in range(FAN)]
            summed = jnp.dot(
                jnp.concatenate(parts, axis=1),
                tiles[index, block],
                preferred_element_type=jnp.float32,
            )
            shifted = summed + biases_ref[index : index + 1, block * WIDTH : (block + 1) * WIDTH]
            held[block] = jnp.clip(shifted, 0.0, CEILING).astype(jnp.bfloat16)

    def to_table(rows, table):
        copy = pltpu.make_async_copy(rows, table, table_sem)
        copy.start()
        copy.wait()


    @pl.when(section == 0)
    def _():
        exchange(
            held, lambda reader: slots_ref[0, reader],
            start_out, 0, first_0, start_send, first_recv.at[0], True,
        )
        full(next_rows, next_row_recv)
        send_rows(1, start_rows, row_send.at[0], start_row_recv)
        pl.semaphore_wait(hello.at[0], 1)
        send_rows(2, start_rows, row_send.at[1], start_row_recv)

    @pl.when(section > 0)
    def _():
        send_rows(section - 1, next_rows, row_send.at[0], next_row_recv)

    for batch in range(1, SECTIONS):

        @pl.when(section == batch)
        def _():
            if batch > 1:
                pl.semaphore_signal(hello.at[batch - 2], inc=1, device_id=(0, me), device_id_type=MESH)
            full(start_rows, start_row_recv)
            to_table(start_rows, start_slots)
            exchange(
                held, lambda reader: start_slots[0, reader],
                start_out, 0, first_in[batch], start_send, first_recv.at[batch], False,
            )

    for load in loads[3:]:
        load.wait()

    def first(batch):
        if batch == 0:
            arrived(first_0, READERS - 1, first_recv.at[0])
        elif batch < PASSED:

            @pl.when(section == 0)
            def _():
                full(first_in[batch], first_recv.at[batch])

            @pl.when(section > 0)
            def _():
                arrived(first_in[batch], READERS - 1, first_recv.at[batch])

        else:
            full(first_in[batch], first_recv.at[batch])
        layer(0, first_in[batch])
        exchange(
            held, lambda reader: slots_ref[1, reader], second_out.at[batch], section,
            second_in[batch], second_send.at[batch], second_recv.at[batch], True,
        )

    def second(batch):
        arrived(second_in[batch], READERS - 1, second_recv.at[batch])
        layer(1, second_in[batch])

        @pl.when(section < last)
        def _():
            if batch < PASSED:
                passed_out[batch] = held[...]
                pltpu.make_async_remote_copy(
                    src_ref=passed_out.at[batch],
                    dst_ref=passed_in[batch],
                    send_sem=pass_send.at[batch],
                    recv_sem=pass_recv.at[batch],
                    device_id=(section + 1, me),
                    device_id_type=MESH,
                ).start()
            else:
                exchange(
                    held, lambda reader: next_slots[0, reader], first_out.at[batch], section + 1,
                    first_in[batch], first_send.at[batch], first_recv.at[batch], False,
                )

        @pl.when(section == last)
        def _():
            for block in range(BLOCKS):
                scaled = held[block].astype(jnp.float32) * (1.0 / CEILING)
                result[batch, :, block * WIDTH : (block + 1) * WIDTH] = scaled.astype(jnp.bfloat16)
            if batch < last:
                pltpu.make_async_remote_copy(
                    src_ref=result.at[batch],
                    dst_ref=landed,
                    send_sem=land_send,
                    recv_sem=land_recv,
                    device_id=(batch, me),
                    device_id_type=MESH,
                ).start()

    @pl.when(section > 0)
    def _():
        for batch in range(PASSED):
            full(passed_in[batch], pass_recv.at[batch])
            exchange(
                passed_in[batch], lambda reader: slots_ref[0, reader], first_out.at[batch], section,
                first_in[batch], first_send.at[batch], first_recv.at[batch], True,
            )

    first(0)

    @pl.when(section == 0)
    def _():
        pl.semaphore_wait(hello.at[1], 1)
        send_rows(3, start_rows, row_send.at[2], start_row_recv)
        to_table(next_rows, next_slots)

    @pl.when(jnp.logical_and(section > 0, section < last))
    def _():
        full(next_rows, next_row_recv)
        to_table(next_rows, next_slots)

    first(1)
    second(0)
    first(2)
    second(1)
    first(3)
    second(2)
    second(3)

    full(slot_rows, row_send.at[0])

    @pl.when(section == 0)
    def _():
        full(slot_rows, row_send.at[1])
        full(slot_rows, row_send.at[2])
        arrived(start_out, READERS - 1, start_send)

    @pl.when(section > 0)
    def _():
        full(start_out, start_send)
        for batch in range(PASSED):
            arrived(first_out.at[batch], READERS - 1, first_send.at[batch])

    for batch in range(SECTIONS):
        arrived(second_out.at[batch], READERS - 1, second_send.at[batch])

    @pl.when(section < last)
    def _():
        for batch in range(SECTIONS):
            if batch < PASSED:
                full(passed_out.at[batch], pass_send.at[batch])
            else:
                full(first_out.at[batch], first_send.at[batch])
        full(landed, land_recv)
        out_ref[...] = landed[...]

    @pl.when(section == last)
    def _():
        full(result.at[pl.ds(0, SECTIONS - 1)], land_send)
        out_ref[...] = result[last]


def per_device(inputs, weights, biases, sources, send_slot):
    slots = send_slot.reshape(2, READERS)
    bf16 = jnp.bfloat16
    pool = (READERS, ROWS, WIDTH)
    dma = pltpu.SemaphoreType.DMA
    return pl.pallas_call(
        kernel,
        out_shape=jax.ShapeDtypeStruct((ROWS, BLOCKS * WIDTH), bf16),
        in_specs=[pl.BlockSpec(memory_space=pltpu.HBM)] * 5,
        out_specs=pl.BlockSpec(memory_space=pltpu.VMEM),
        scratch_shapes=[
            pltpu.VMEM((BLOCKS, ROWS, WIDTH), bf16),
            *[pltpu.VMEM(pool, bf16)] * (2 * SECTIONS),
            *[pltpu.VMEM((BLOCKS, ROWS, WIDTH), bf16)] * PASSED,
            pltpu.VMEM((PASSED, BLOCKS, ROWS, WIDTH), bf16),
            dma((PASSED,)),
            dma((PASSED,)),
            pltpu.VMEM((SECTIONS, *pool), bf16),
            pltpu.VMEM((SECTIONS, *pool), bf16),
            pltpu.VMEM(pool, bf16),
            pltpu.VMEM(inputs.shape, bf16),
            pltpu.VMEM(weights.shape, bf16),
            pltpu.VMEM(biases.shape, jnp.float32),
            pltpu.SMEM(sources.shape, jnp.int32),
            pltpu.SMEM(slots.shape, jnp.int32),
            pltpu.VMEM(slots.shape, jnp.int32),
            pltpu.VMEM(slots.shape, jnp.int32),
            pltpu.VMEM(slots.shape, jnp.int32),
            pltpu.SMEM(slots.shape, jnp.int32),
            pltpu.SMEM(slots.shape, jnp.int32),
            pltpu.VMEM((SECTIONS, ROWS, BLOCKS * WIDTH), bf16),
            pltpu.VMEM((ROWS, BLOCKS * WIDTH), bf16),
            dma((SECTIONS,)),
            dma((SECTIONS,)),
            dma((SECTIONS,)),
            dma((SECTIONS,)),
            dma(()),
            dma((6,)),
            dma((SECTIONS - 1,)),
            dma(()),
            dma(()),
            dma(()),
            dma(()),
            dma(()),
            pltpu.SemaphoreType.REGULAR((2,)),
        ],
        compiler_params=pltpu.CompilerParams(
            collective_id=0, has_side_effects=True, vmem_limit_bytes=60 * 2**20
        ),
        cost_estimate=pl.CostEstimate(flops=2**28, bytes_accessed=2**23, transcendentals=0),
    )(inputs, weights, biases, sources, slots)


def solution(mesh):
    placed = (
        P("segment", "blk"),
        P("segment", "blk", None, None),
        P("segment", "blk"),
        P("segment", "blk", None),
        P("segment", "blk", None, None),
    )
    return jax.shard_map(
        per_device, mesh=mesh, in_specs=placed, out_specs=P("segment", "blk"), check_vma=False
    )
```
